32 devices in a mesh: row: 4 (over y, x), col: 8 (over z, core).
Axes of the slice: x: 2, y: 2, z: 4, core: 2. Of those that a mesh axis runs over, the one named last changes fastest.
Arguments:
- precond: float32 [8, 8192, 8192], P(None, 'row', 'col'), may hold values from -6 to 6
- out_factors: bfloat16 [1536, 8192], P('col', 'row'), may hold values from -6 to 6
- in_factors: bfloat16 [1536, 8192], P('row', 'col'), may hold values from -6 to 6
- token_mask: int32 [1536], replicated, may hold values 0 or 1
- seq_ids: int32 [1536], replicated, may hold values from 0 to 3, never falling along the last dimension, each value on 1 to 576 neighbouring positions
- query_ids: int32 [8], replicated, may hold values from 0 to 7, each once
Outputs:
- scores: float32 [8, 4], replicated
The draws below stay inside these ranges and needn't reach their ends.
Inputs may be any that keep to these rules, and one draw needn't show every extreme that they name: seq_ids never falls along the tokens; each sequence has 1 to 576 tokens. query_ids names each query once.
All inputs are finite; a program needn't handle non-finite values.
Results may differ from the reference program's by a relative error of at most 0.0003.
Values may be sent and summed in bfloat16 or wider, within the bound.
A program may use at most 128 MiB of HBM per device.

```python
import math
import jax
import jax.numpy as jnp
import numpy as np
from jax import lax

DOUT = 8192
DIN = 8192
QUERIES = 8
SEQ = 4
LEN = 384
TOKENS = 1536
MOST = 576


def with_ends(array, rng, smallest, high):
    shape = array.shape
    spot = [jax.random.randint(jax.random.fold_in(rng, axis), (), 0, shape[axis]) for axis in range(len(shape))]
    array = array.at[tuple(spot)].set(smallest)
    longest = shape.index(max(shape))
    spot[longest] = (spot[longest] + 1) % shape[longest]
    return array.at[tuple(spot)].set(high)


def levels(rng, shape, split, smallest, top_value):
    def one(axis_at, parts):
        heights = jax.random.uniform(jax.random.fold_in(jax.random.fold_in(rng, 6), axis_at), (parts,), jnp.float32, smallest / len(split), top_value / len(split))
        return jnp.repeat(jnp.exp(heights), shape[axis_at] // parts).reshape((-1,) + (1,) * (len(shape) - axis_at - 1))

    level = one(*split[0])
    for cut in split[1:]:
        level = level * one(*cut)
    return level


def split_up(number_of, total, limit, lean):
    loads = [(1 << 20) // math.isqrt(grade ** lean) + 1 for grade in range(2, number_of + 1)]
    spare, counts = total - limit - (number_of - 1), [1] * (number_of - 1)
    while spare > 0:
        free = [i for i in range(number_of - 1) if counts[i] < limit]
        pool, left = sum([loads[i] for i in free]), spare
        for i in free:
            addition = min(limit - counts[i], max(1, left * loads[i] // pool), spare)
            counts[i] = counts[i] + addition
            spare = spare - addition
    return np.array([limit] + counts)


def ragged_sizes(rng, number_of, total, limit, skew):
    if number_of == 2:
        one = jax.random.randint(rng, (), max(1, total - limit), min(limit, total - 1) + 1)
        return jnp.stack([one, total - one])
    tallies = jnp.asarray(split_up(number_of, total, limit, skew), jnp.int32)
    pairs = (number_of - 1) // 2
    donor, sink = tallies[1:1 + 2 * pairs:2], tallies[2:2 + 2 * pairs:2]
    room = jnp.minimum(donor - 1, limit - sink)
    shifted = jax.random.randint(jax.random.fold_in(rng, 1), (pairs,), 0, 1 << 20) % (room + 1)
    tallies = tallies.at[1:1 + 2 * pairs:2].set(donor - shifted).at[2:2 + 2 * pairs:2].set(sink + shifted)
    return tallies[jax.random.permutation(jax.random.fold_in(rng, 2), number_of)]


def gaussian(stream_key, dims, deviation, bound, pieces=(), kind=jnp.bfloat16):
    factor_of = levels(stream_key, dims, pieces, -0.22, 0.18) if pieces else 1.0
    drawn = jax.random.normal(stream_key, dims, jnp.float32) * deviation * factor_of
    return jnp.minimum(jnp.maximum(drawn, -bound), bound).astype(kind)


def setup_inputs(seed: int = 0) -> dict:
    keys = jax.random.split(jax.random.key(seed), 7)
    return {
        "precond": gaussian(keys[0], (QUERIES, DOUT, DIN), 1.0, 6.0, ((1, 4), (2, 8)), jnp.float32),
        "out_factors": gaussian(keys[1], (TOKENS, DOUT), 1.0, 6.0, ((0, 8), (1, 4))),
        "in_factors": gaussian(keys[2], (TOKENS, DIN), 1.0, 6.0, ((0, 4), (1, 8))),
        "token_mask": with_ends((jax.random.randint(keys[3], (TOKENS,), 0, 4) < 3).astype(jnp.int32), jax.random.fold_in(keys[3], 1), 0, 1),
        "seq_ids": jnp.searchsorted(jnp.cumsum(ragged_sizes(keys[4], SEQ, TOKENS, MOST, 0)), jnp.arange(TOKENS), side="right").astype(jnp.int32),
        "query_ids": jax.random.permutation(keys[5], QUERIES).astype(jnp.int32),
    }


def reference(precond, out_factors, in_factors, token_mask, seq_ids, query_ids):
    weight = token_mask.astype(jnp.float32)[:, None] * (seq_ids[:, None] == jnp.arange(SEQ, dtype=jnp.int32)[None, :]).astype(jnp.float32)
    out_wide = out_factors.astype(jnp.float32)
    in_wide = in_factors.astype(jnp.float32)

    def one_query(query_grad):
        mapped = jnp.dot(in_wide, query_grad.T, precision=lax.Precision.HIGHEST)
        per_token = lax.optimization_barrier(jnp.sum(mapped * out_wide, axis=1))
        return jnp.dot(per_token, weight, precision=lax.Precision.HIGHEST)
    raw = lax.map(one_query, precond)
    select = (query_ids[:, None] == jnp.arange(QUERIES, dtype=jnp.int32)[None, :]).astype(jnp.float32)
    scale = 1.0 / math.sqrt(DOUT * DIN * LEN)
    return jnp.dot(select, raw, precision=lax.Precision.HIGHEST) * scale
```

```python
import functools
import math

import jax
import jax.numpy as jnp
from jax import lax
from jax.experimental import pallas as pl
from jax.experimental.pallas import tpu as pltpu
from jax.sharding import PartitionSpec as P

DOUT = 8192
DIN = 8192
SEQ = 4
LEN = 384
SCALE = 1.0 / math.sqrt(DOUT * DIN * LEN)
MESH = pl.DeviceIdType.MESH
MOST = 576
CHUNKS = 8
HALVES = 2
SLOTS = 6
AHEAD = 3
NZ = 4
ORDER = [(0, 0), (1, 0), (2, 0), (3, 0), (0, 1), (1, 1), (2, 1), (3, 1),
         (4, 0), (4, 1), (5, 0), (5, 1), (6, 0), (6, 1), (7, 0), (7, 1)]
RELAY = {2: 2, 3: 3, 4: 4, 6: 5, 9: 6, 12: 7}


def table(n, values):
    got = jnp.int32(values[0])
    for at, value in enumerate(values[1:], 1):
        got = jnp.where(n == at, jnp.int32(value), got)
    return got


def windows(tokens):
    got = []
    for s in range(SEQ):
        first = max(0, tokens - (SEQ - s) * MOST) // 128 * 128
        last = min(tokens, -(-(s + 1) * MOST // 128) * 128)
        got.append((first, last - first))
    return got


def fused(code_ref, ids_ref, out_ref, in_ref, p_ref, res_ref,
          o_buf, o_t, i_buf0, i_buf1, in_w, p_buf, g_buf, wcol, acc_ref, x1, x2,
          p_sem, o_recv, own_sem, sib_sem, fwd_sem, i_recv, i_send,
          x1_recv, x1_send, x2_recv, x2_send):
    nq = p_ref.shape[0]
    rows_n, cols_n = 4, 2 * NZ
    tb, wide = out_ref.shape
    ib, deep = in_ref.shape
    ci = wide // CHUNKS
    cj = deep // HALVES
    row = lax.axis_index("row")
    col = lax.axis_index("col")
    z = col // 2
    core = col % 2
    i_bufs = (i_buf0, i_buf1)

    barrier = pltpu.get_barrier_semaphore()
    for d in range(1, cols_n):
        pl.semaphore_signal(barrier, inc=1, device_id={"col": lax.rem(col + d, cols_n)}, device_id_type=MESH)
    for d in range(1, rows_n):
        pl.semaphore_signal(barrier, inc=1, device_id={"row": lax.rem(row + d, rows_n)}, device_id_type=MESH)

    def p_copy(n):
        k = table(n, [o[0] for o in ORDER])
        h = table(n, [o[1] for o in ORDER])
        slot = lax.rem(n, SLOTS)
        return pltpu.make_async_copy(
            p_ref.at[:, pl.ds(pl.multiple_of(k * ci, ci), ci), pl.ds(pl.multiple_of(h * cj, cj), cj)],
            p_buf.at[slot], p_sem.at[slot])

    for n in range(SLOTS):
        p_copy(jnp.int32(n)).start()
    pl.semaphore_wait(barrier, cols_n - 1 + rows_n - 1)

    def o_rows(src):
        return pl.ds(pl.multiple_of(src * tb, 64), tb)

    def own_copy(k, d):
        dst = lax.rem(z + d, NZ)
        return pltpu.make_async_remote_copy(
            src_ref=out_ref.at[:, pl.ds(pl.multiple_of(k * ci, ci), ci)],
            dst_ref=o_buf.at[k, o_rows(col), :],
            send_sem=own_sem.at[k, d], recv_sem=o_recv.at[k, col],
            device_id={"col": dst * 2 + core}, device_id_type=MESH)

    def direct(d):
        dst = lax.rem(z + d, NZ)
        return jnp.abs(dst - z) < NZ - 1

    def own_sib(k):
        return pltpu.make_async_remote_copy(
            src_ref=out_ref.at[:, pl.ds(pl.multiple_of(k * ci, ci), ci)],
            dst_ref=o_buf.at[k, o_rows(col), :],
            send_sem=sib_sem.at[k, 0], recv_sem=o_recv.at[k, col],
            device_id={"col": z * 2 + 1 - core}, device_id_type=MESH)

    def pass_sib(k, d):
        src = lax.rem(z + d, NZ) * 2 + core
        return pltpu.make_async_remote_copy(
            src_ref=o_buf.at[k, o_rows(src), :], dst_ref=o_buf.at[k, o_rows(src), :],
            send_sem=sib_sem.at[k, d], recv_sem=o_recv.at[k, src],
            device_id={"col": z * 2 + 1 - core}, device_id_type=MESH)

    def ends(d):
        src = lax.rem(z + d, NZ)
        return ((z == NZ - 2) & (src == 0)) | ((z == 1) & (src == NZ - 1))

    def pass_end(k, d):
        zs = lax.rem(z + d, NZ)
        src = zs * 2 + core
        return pltpu.make_async_remote_copy(
            src_ref=o_buf.at[k, o_rows(src), :], dst_ref=o_buf.at[k, o_rows(src), :],
            send_sem=fwd_sem.at[k], recv_sem=o_recv.at[k, src],
            device_id={"col": (NZ - 1 - zs) * 2 + core}, device_id_type=MESH)

    def o_arrived(k, src):
        pltpu.make_async_remote_copy(
            src_ref=o_buf.at[k, o_rows(src), :], dst_ref=o_buf.at[k, o_rows(src), :],
            send_sem=fwd_sem.at[k], recv_sem=o_recv.at[k, src],
            device_id={"col": z * 2 + 1 - core}, device_id_type=MESH).wait_recv()

    def in_copy(h, d):
        return pltpu.make_async_remote_copy(
            src_ref=in_ref.at[:, pl.ds(h * cj, cj)],
            dst_ref=i_bufs[h].at[pl.ds(pl.multiple_of(row * ib, ib), ib), :],
            send_sem=i_send.at[h, d], recv_sem=i_recv.at[h, row],
            device_id={"row": lax.rem(row + d, rows_n)}, device_id_type=MESH)

    def in_arrived(h, d):
        src = lax.rem(row + d, rows_n)
        pltpu.make_async_remote_copy(
            src_ref=in_ref.at[:, pl.ds(h * cj, cj)],
            dst_ref=i_bufs[h].at[pl.ds(pl.multiple_of(src * ib, ib), ib), :],
            send_sem=i_send.at[h, d], recv_sem=i_recv.at[h, src],
            device_id={"row": src}, device_id_type=MESH).wait_recv()

    def send_own(k):
        own_sib(k).start()
        for d in range(1, NZ):
            @pl.when(direct(d))
            def _():
                own_copy(k, d).start()

    def relay(k):
        for d in range(1, NZ):
            src = lax.rem(z + d, NZ) * 2 + core
            o_arrived(k, src)

            @pl.when(ends(d))
            def _():
                pass_end(k, d).start()
            pass_sib(k, d).start()

        @pl.when(k + AHEAD < CHUNKS)
        def _():
            send_own(k + AHEAD)

    for k in range(AHEAD):
        send_own(jnp.int32(k))
        if k < HALVES:
            for d in range(1, rows_n):
                in_copy(k, d).start()

    for k in range(CHUNKS):
        o_buf[k, o_rows(col), :] = out_ref[:, k * ci:(k + 1) * ci]
    for h in range(HALVES):
        i_bufs[h][pl.ds(pl.multiple_of(row * ib, ib), ib), :] = in_ref[:, h * cj:(h + 1) * cj]
    wcol[...] = jnp.transpose(code_ref[...])
    acc_ref[...] = jnp.zeros_like(acc_ref)

    spans = windows(code_ref.shape[1])
    places = [sum(w[1] for w in spans[:s]) for s in range(SEQ)]

    def weigh(h):
        for d in range(1, rows_n):
            in_arrived(h, d)
        for s in range(SEQ):
            first, size = spans[s]
            mine = (wcol[first:first + size, 0:1] == float(s)).astype(jnp.float32)
            in_w[h, places[s]:places[s] + size] = i_bufs[h][first:first + size, :] * mine.astype(jnp.bfloat16)

    relay(jnp.int32(0))
    relay(jnp.int32(1))
    weigh(0)

    def unit(n, carry):
        k = table(n, [o[0] for o in ORDER])
        h = table(n, [o[1] for o in ORDER])
        step = table(n, [RELAY.get(i, 0) for i in range(len(ORDER))])

        @pl.when(step > 0)
        def _():
            relay(step)

        @pl.when(n == 4)
        def _():
            weigh(1)

        @pl.when(h == 0)
        def _():
            for zz in range(NZ):
                o_arrived(k, zz * 2 + 1 - core)
            o_t[k] = jnp.transpose(o_buf[k])

        for s in range(SEQ):
            first, size = spans[s]
            g_buf[s] = jnp.dot(o_t[k, :, first:first + size], in_w[h, places[s]:places[s] + size, :],
                               preferred_element_type=jnp.float32)

        p_copy(n).wait()
        slot = lax.rem(n, SLOTS)

        def strip(r, accs):
            accs = list(accs)
            at = pl.ds(pl.multiple_of(r * 8, 8), 8)
            for lane in range(cj // 128):
                here = pl.ds(lane * 128, 128)
                gs = [g_buf[s, at, here] for s in range(SEQ)]
                for q in range(nq):
                    pq = p_buf[slot, q, at, here]
                    for s in range(SEQ):
                        accs[s * nq + q] = accs[s * nq + q] + pq * gs[s]
            return tuple(accs)

        accs = lax.fori_loop(0, ci // 8, strip, tuple(acc_ref[i] for i in range(SEQ * nq)))
        for i in range(SEQ * nq):
            acc_ref[i] = accs[i]

        @pl.when(n + SLOTS < len(ORDER))
        def _():
            p_copy(n + SLOTS).start()
        return carry

    lax.fori_loop(0, len(ORDER), unit, 0)

    def share(buf, recv, send, name, me, count, value):
        buf[me] = value
        for d in range(1, count):
            pltpu.make_async_remote_copy(
                src_ref=buf.at[me], dst_ref=buf.at[me], send_sem=send.at[d], recv_sem=recv.at[me],
                device_id={name: lax.rem(me + d, count)}, device_id_type=MESH).start()
        for d in range(1, count):
            src = lax.rem(me + d, count)
            pltpu.make_async_remote_copy(
                src_ref=buf.at[src], dst_ref=buf.at[src], send_sem=send.at[d], recv_sem=recv.at[src],
                device_id={name: src}, device_id_type=MESH).wait_recv()
        total = buf[0]
        for i in range(1, count):
            total = total + buf[i]
        return total

    def sent(buf, recv, send, name, me, count):
        for d in range(1, count):
            pltpu.make_async_remote_copy(
                src_ref=buf.at[me], dst_ref=buf.at[me], send_sem=send.at[d], recv_sem=recv.at[me],
                device_id={name: lax.rem(me + d, count)}, device_id_type=MESH).wait_send()

    mine = jnp.sum(acc_ref[...], axis=1)
    total = share(x1, x1_recv, x1_send, "col", col, cols_n, mine)
    total = share(x2, x2_recv, x2_send, "row", row, rows_n, total)
    sums = jnp.sum(total, axis=1, keepdims=True)
    lanes = lax.broadcasted_iota(jnp.int32, (nq, 128), 1)
    raw = jnp.zeros((nq, 128), jnp.float32)
    for s in range(SEQ):
        raw = raw + jnp.where(lanes == s, sums[s * nq:(s + 1) * nq], 0.0)
    picked = jnp.zeros((nq, 128), jnp.float32)
    for q in range(nq):
        picked = picked + jnp.where(ids_ref[...] == q, raw[q:q + 1], 0.0)
    res_ref[...] = picked * SCALE

    def left(k, carry):
        own_sib(k).wait_send()
        for d in range(1, NZ):
            @pl.when(direct(d))
            def _():
                own_copy(k, d).wait_send()

            @pl.when(ends(d))
            def _():
                pass_end(k, d).wait_send()
            pass_sib(k, d).wait_send()
        return carry

    lax.fori_loop(0, CHUNKS, left, 0)
    for h in range(HALVES):
        for d in range(1, rows_n):
            in_copy(h, d).wait_send()
    sent(x1, x1_recv, x1_send, "col", col, cols_n)
    sent(x2, x2_recv, x2_send, "row", row, rows_n)


def local_fused(precond, out_factors, in_factors, token_mask, seq_ids, query_ids):
    nq, wide, deep = precond.shape
    tokens = seq_ids.shape[0]
    code = jnp.where(token_mask == 1, seq_ids, -1).astype(jnp.float32)
    code = jnp.broadcast_to(code[None, :], (8, tokens))
    ids = jnp.broadcast_to(query_ids[:, None], (nq, 128))
    ci, cj = wide // CHUNKS, deep // HALVES
    held = sum(size for _, size in windows(tokens))
    vmem = pl.BlockSpec(memory_space=pltpu.VMEM)
    dma = pltpu.SemaphoreType.DMA
    res = pl.pallas_call(
        fused,
        out_shape=jax.ShapeDtypeStruct((nq, 128), jnp.float32),
        in_specs=[vmem, vmem, vmem, vmem, pl.BlockSpec(memory_space=pl.ANY)],
        out_specs=vmem,
        scratch_shapes=[
            pltpu.VMEM((CHUNKS, tokens, ci), jnp.bfloat16),
            pltpu.VMEM((CHUNKS, ci, tokens), jnp.bfloat16),
            pltpu.VMEM((tokens, cj), jnp.bfloat16),
            pltpu.VMEM((tokens, cj), jnp.bfloat16),
            pltpu.VMEM((HALVES, held, cj), jnp.bfloat16),
            pltpu.VMEM((SLOTS, nq, ci, cj), jnp.float32),
            pltpu.VMEM((SEQ, ci, cj), jnp.float32),
            pltpu.VMEM((tokens, 8), jnp.float32),
            pltpu.VMEM((SEQ * nq, 8, 128), jnp.float32),
            pltpu.VMEM((2 * NZ, SEQ * nq, 128), jnp.float32),
            pltpu.VMEM((4, SEQ * nq, 128), jnp.float32),
            dma((SLOTS,)), dma((CHUNKS, 2 * NZ)), dma((CHUNKS, NZ)), dma((CHUNKS, NZ)),
            dma((CHUNKS,)), dma((HALVES, 4)), dma((HALVES, 4)),
            dma((2 * NZ,)), dma((2 * NZ,)), dma((4,)), dma((4,)),
        ],
        compiler_params=pltpu.CompilerParams(
            collective_id=0, has_side_effects=True, vmem_limit_bytes=60 << 20),
        cost_estimate=pl.CostEstimate(
            flops=2 * wide * deep * (held + SEQ * nq), bytes_accessed=4 * nq * wide * deep, transcendentals=0),
    )(code, ids, out_factors, in_factors, precond)
    return res[:, :SEQ]


def local_plain(precond, out_factors, in_factors, token_mask, seq_ids, query_ids):
    out_whole = lax.all_gather(out_factors, "col", axis=0, tiled=True)
    in_whole = lax.all_gather(in_factors, "row", axis=0, tiled=True)

    def one_sequence(s):
        weight = ((seq_ids == s) & (token_mask == 1)).astype(jnp.bfloat16)
        outer = lax.dot_general(out_whole, in_whole * weight[:, None], (((0,), (0,)), ((), ())),
                                preferred_element_type=jnp.float32)
        return jnp.sum(precond * outer[None], axis=(1, 2))

    total = lax.map(one_sequence, jnp.arange(SEQ, dtype=jnp.int32))
    raw = lax.psum(total, ("row", "col")).T
    select = (query_ids[:, None] == jnp.arange(raw.shape[0], dtype=jnp.int32)[None, :]).astype(jnp.float32)
    return jnp.dot(select, raw, precision=lax.Precision.HIGHEST) * SCALE


def solution(mesh):
    placed = (P(None, "row", "col"), P("col", "row"), P("row", "col"), P(), P(), P())
    small = mesh.shape["row"] == 4 and mesh.shape["col"] == 2 * NZ
    return jax.shard_map(local_fused if small else local_plain, mesh=mesh, in_specs=placed,
                         out_specs=P(), check_vma=False)
```

```python
import functools
import math

import jax
import jax.numpy as jnp
from jax import lax
from jax.experimental import pallas as pl
from jax.experimental.pallas import tpu as pltpu
from jax.sharding import PartitionSpec as P

DOUT = 8192
DIN = 8192
SEQ = 4
LEN = 384
SCALE = 1.0 / math.sqrt(DOUT * DIN * LEN)
MESH = pl.DeviceIdType.MESH
MOST = 576
CHUNKS = 8
HALVES = 2
SLOTS = 6
AHEAD = 4
NZ = 4
ORDER = [(0, 0), (1, 0), (2, 0), (3, 0), (0, 1), (1, 1), (2, 1), (3, 1),
         (4, 0), (4, 1), (5, 0), (5, 1), (6, 0), (6, 1), (7, 0), (7, 1)]
RELAY = {2: 2, 3: 3, 4: 4, 6: 5, 9: 6, 12: 7}


def table(n, values):
    got = jnp.int32(values[0])
    for at, value in enumerate(values[1:], 1):
        got = jnp.where(n == at, jnp.int32(value), got)
    return got


def windows(tokens):
    got = []
    for s in range(SEQ):
        first = max(0, tokens - (SEQ - s) * MOST) // 128 * 128
        last = min(tokens, -(-(s + 1) * MOST // 128) * 128)
        got.append((first, last - first))
    return got


def fused(code_ref, ids_ref, out_ref, in_ref, p_ref, res_ref,
          o_buf, o_t, i_buf0, i_buf1, in_w, p_buf, g_buf, wcol, acc_ref, x1, x2,
          p_sem, o_recv, own_sem, sib_sem, fwd_sem, i_recv, i_send,
          x1_recv, x1_send, x2_recv, x2_send):
    nq = p_ref.shape[0]
    rows_n, cols_n = 4, 2 * NZ
    tb, wide = out_ref.shape
    ib, deep = in_ref.shape
    ci = wide // CHUNKS
    cj = deep // HALVES
    row = lax.axis_index("row")
    col = lax.axis_index("col")
    z = col // 2
    core = col % 2
    i_bufs = (i_buf0, i_buf1)

    barrier = pltpu.get_barrier_semaphore()
    for d in range(1, cols_n):
        pl.semaphore_signal(barrier, inc=1, device_id={"col": lax.rem(col + d, cols_n)}, device_id_type=MESH)
    for d in range(1, rows_n):
        pl.semaphore_signal(barrier, inc=1, device_id={"row": lax.rem(row + d, rows_n)}, device_id_type=MESH)

    def p_copy(n):
        k = table(n, [o[0] for o in ORDER])
        h = table(n, [o[1] for o in ORDER])
        slot = lax.rem(n, SLOTS)
        return pltpu.make_async_copy(
            p_ref.at[:, pl.ds(pl.multiple_of(k * ci, ci), ci), pl.ds(pl.multiple_of(h * cj, cj), cj)],
            p_buf.at[slot], p_sem.at[slot])

    for n in range(SLOTS):
        p_copy(jnp.int32(n)).start()
    pl.semaphore_wait(barrier, cols_n - 1 + rows_n - 1)

    def o_rows(src):
        return pl.ds(pl.multiple_of(src * tb, 64), tb)

    def own_copy(k, d):
        dst = lax.rem(z + d, NZ)
        return pltpu.make_async_remote_copy(
            src_ref=out_ref.at[:, pl.ds(pl.multiple_of(k * ci, ci), ci)],
            dst_ref=o_buf.at[k, o_rows(col), :],
            send_sem=own_sem.at[k, d], recv_sem=o_recv.at[k, col],
            device_id={"col": dst * 2 + core}, device_id_type=MESH)

    def direct(d):
        dst = lax.rem(z + d, NZ)
        return jnp.abs(dst - z) < NZ - 1

    def own_sib(k):
        return pltpu.make_async_remote_copy(
            src_ref=out_ref.at[:, pl.ds(pl.multiple_of(k * ci, ci), ci)],
            dst_ref=o_buf.at[k, o_rows(col), :],
            send_sem=sib_sem.at[k, 0], recv_sem=o_recv.at[k, col],
            device_id={"col": z * 2 + 1 - core}, device_id_type=MESH)

    def pass_sib(k, d):
        src = lax.rem(z + d, NZ) * 2 + core
        return pltpu.make_async_remote_copy(
            src_ref=o_buf.at[k, o_rows(src), :], dst_ref=o_buf.at[k, o_rows(src), :],
            send_sem=sib_sem.at[k, d], recv_sem=o_recv.at[k, src],
            device_id={"col": z * 2 + 1 - core}, device_id_type=MESH)

    def ends(d):
        src = lax.rem(z + d, NZ)
        return ((z == NZ - 2) & (src == 0)) | ((z == 1) & (src == NZ - 1))

    def pass_end(k, d):
        zs = lax.rem(z + d, NZ)
        src = zs * 2 + core
        return pltpu.make_async_remote_copy(
            src_ref=o_buf.at[k, o_rows(src), :], dst_ref=o_buf.at[k, o_rows(src), :],
            send_sem=fwd_sem.at[k], recv_sem=o_recv.at[k, src],
            device_id={"col": (NZ - 1 - zs) * 2 + core}, device_id_type=MESH)

    def o_arrived(k, src):
        pltpu.make_async_remote_copy(
            src_ref=o_buf.at[k, o_rows(src), :], dst_ref=o_buf.at[k, o_rows(src), :],
            send_sem=fwd_sem.at[k], recv_sem=o_recv.at[k, src],
            device_id={"col": z * 2 + 1 - core}, device_id_type=MESH).wait_recv()

    def in_copy(h, d):
        return pltpu.make_async_remote_copy(
            src_ref=in_ref.at[:, pl.ds(h * cj, cj)],
            dst_ref=i_bufs[h].at[pl.ds(pl.multiple_of(row * ib, ib), ib), :],
            send_sem=i_send.at[h, d], recv_sem=i_recv.at[h, row],
            device_id={"row": lax.rem(row + d, rows_n)}, device_id_type=MESH)

    def in_arrived(h, d):
        src = lax.rem(row + d, rows_n)
        pltpu.make_async_remote_copy(
            src_ref=in_ref.at[:, pl.ds(h * cj, cj)],
            dst_ref=i_bufs[h].at[pl.ds(pl.multiple_of(src * ib, ib), ib), :],
            send_sem=i_send.at[h, d], recv_sem=i_recv.at[h, src],
            device_id={"row": src}, device_id_type=MESH).wait_recv()

    def send_own(k):
        own_sib(k).start()
        for d in range(1, NZ):
            @pl.when(direct(d))
            def _():
                own_copy(k, d).start()

    def relay(k):
        for d in range(1, NZ):
            src = lax.rem(z + d, NZ) * 2 + core
            o_arrived(k, src)

            @pl.when(ends(d))
            def _():
                pass_end(k, d).start()
            pass_sib(k, d).start()

        @pl.when(k + AHEAD < CHUNKS)
        def _():
            send_own(k + AHEAD)

    for k in range(AHEAD):
        send_own(jnp.int32(k))
        if k < HALVES:
            for d in range(1, rows_n):
                in_copy(k, d).start()

    for k in range(CHUNKS):
        o_buf[k, o_rows(col), :] = out_ref[:, k * ci:(k + 1) * ci]
    for h in range(HALVES):
        i_bufs[h][pl.ds(pl.multiple_of(row * ib, ib), ib), :] = in_ref[:, h * cj:(h + 1) * cj]
    wcol[...] = jnp.transpose(code_ref[...])
    acc_ref[...] = jnp.zeros_like(acc_ref)

    spans = windows(code_ref.shape[1])
    places = [sum(w[1] for w in spans[:s]) for s in range(SEQ)]

    def weigh(h):
        for d in range(1, rows_n):
            in_arrived(h, d)
        for s in range(SEQ):
            first, size = spans[s]
            mine = (wcol[first:first + size, 0:1] == float(s)).astype(jnp.float32)
            in_w[h, places[s]:places[s] + size] = i_bufs[h][first:first + size, :] * mine.astype(jnp.bfloat16)

    relay(jnp.int32(0))
    relay(jnp.int32(1))
    weigh(0)

    def unit(n, carry):
        k = table(n, [o[0] for o in ORDER])
        h = table(n, [o[1] for o in ORDER])
        step = table(n, [RELAY.get(i, 0) for i in range(len(ORDER))])

        @pl.when(step > 0)
        def _():
            relay(step)

        @pl.when(n == 4)
        def _():
            weigh(1)

        @pl.when(h == 0)
        def _():
            for zz in range(NZ):
                o_arrived(k, zz * 2 + 1 - core)
            o_t[k] = jnp.transpose(o_buf[k])

        for s in range(SEQ):
            first, size = spans[s]
            g_buf[s] = jnp.dot(o_t[k, :, first:first + size], in_w[h, places[s]:places[s] + size, :],
                               preferred_element_type=jnp.float32)

        p_copy(n).wait()
        slot = lax.rem(n, SLOTS)

        def strip(r, accs):
            accs = list(accs)
            for part in range(4 * cj // 128):
                at = pl.ds(pl.multiple_of(r * 32 + part % 4 * 8, 8), 8)
                here = pl.ds(part // 4 * 128, 128)
                gs = [g_buf[s, at, here] for s in range(SEQ)]
                for q in range(nq):
                    pq = p_buf[slot, q, at, here]
                    for s in range(SEQ):
                        accs[s * nq + q] = accs[s * nq + q] + pq * gs[s]
            return tuple(accs)

        accs = lax.fori_loop(0, ci // 32, strip, tuple(acc_ref[i] for i in range(SEQ * nq)))
        for i in range(SEQ * nq):
            acc_ref[i] = accs[i]

        @pl.when(n + SLOTS < len(ORDER))
        def _():
            p_copy(n + SLOTS).start()
        return carry

    lax.fori_loop(0, len(ORDER), unit, 0)

    def share(buf, recv, send, name, me, count, value):
        buf[me] = value
        for d in range(1, count):
            pltpu.make_async_remote_copy(
                src_ref=buf.at[me], dst_ref=buf.at[me], send_sem=send.at[d], recv_sem=recv.at[me],
                device_id={name: lax.rem(me + d, count)}, device_id_type=MESH).start()
        for d in range(1, count):
            src = lax.rem(me + d, count)
            pltpu.make_async_remote_copy(
                src_ref=buf.at[src], dst_ref=buf.at[src], send_sem=send.at[d], recv_sem=recv.at[src],
                device_id={name: src}, device_id_type=MESH).wait_recv()
        total = buf[0]
        for i in range(1, count):
            total = total + buf[i]
        return total

    def sent(buf, recv, send, name, me, count):
        for d in range(1, count):
            pltpu.make_async_remote_copy(
                src_ref=buf.at[me], dst_ref=buf.at[me], send_sem=send.at[d], recv_sem=recv.at[me],
                device_id={name: lax.rem(me + d, count)}, device_id_type=MESH).wait_send()

    mine = jnp.sum(acc_ref[...], axis=1)
    total = share(x1, x1_recv, x1_send, "col", col, cols_n, mine)
    total = share(x2, x2_recv, x2_send, "row", row, rows_n, total)
    sums = jnp.sum(total, axis=1, keepdims=True)
    lanes = lax.broadcasted_iota(jnp.int32, (nq, 128), 1)
    raw = jnp.zeros((nq, 128), jnp.float32)
    for s in range(SEQ):
        raw = raw + jnp.where(lanes == s, sums[s * nq:(s + 1) * nq], 0.0)
    picked = jnp.zeros((nq, 128), jnp.float32)
    for q in range(nq):
        picked = picked + jnp.where(ids_ref[...] == q, raw[q:q + 1], 0.0)
    res_ref[...] = picked * SCALE

    def left(k, carry):
        own_sib(k).wait_send()
        for d in range(1, NZ):
            @pl.when(direct(d))
            def _():
                own_copy(k, d).wait_send()

            @pl.when(ends(d))
            def _():
                pass_end(k, d).wait_send()
            pass_sib(k, d).wait_send()
        return carry

    lax.fori_loop(0, CHUNKS, left, 0)
    for h in range(HALVES):
        for d in range(1, rows_n):
            in_copy(h, d).wait_send()
    sent(x1, x1_recv, x1_send, "col", col, cols_n)
    sent(x2, x2_recv, x2_send, "row", row, rows_n)


def local_fused(precond, out_factors, in_factors, token_mask, seq_ids, query_ids):
    nq, wide, deep = precond.shape
    tokens = seq_ids.shape[0]
    code = jnp.where(token_mask == 1, seq_ids, -1).astype(jnp.float32)
    code = jnp.broadcast_to(code[None, :], (8, tokens))
    ids = jnp.broadcast_to(query_ids[:, None], (nq, 128))
    ci, cj = wide // CHUNKS, deep // HALVES
    held = sum(size for _, size in windows(tokens))
    vmem = pl.BlockSpec(memory_space=pltpu.VMEM)
    dma = pltpu.SemaphoreType.DMA
    res = pl.pallas_call(
        fused,
        out_shape=jax.ShapeDtypeStruct((nq, 128), jnp.float32),
        in_specs=[vmem, vmem, vmem, vmem, pl.BlockSpec(memory_space=pl.ANY)],
        out_specs=vmem,
        scratch_shapes=[
            pltpu.VMEM((CHUNKS, tokens, ci), jnp.bfloat16),
            pltpu.VMEM((CHUNKS, ci, tokens), jnp.bfloat16),
            pltpu.VMEM((tokens, cj), jnp.bfloat16),
            pltpu.VMEM((tokens, cj), jnp.bfloat16),
            pltpu.VMEM((HALVES, held, cj), jnp.bfloat16),
            pltpu.VMEM((SLOTS, nq, ci, cj), jnp.float32),
            pltpu.VMEM((SEQ, ci, cj), jnp.float32),
            pltpu.VMEM((tokens, 8), jnp.float32),
            pltpu.VMEM((SEQ * nq, 8, 128), jnp.float32),
            pltpu.VMEM((2 * NZ, SEQ * nq, 128), jnp.float32),
            pltpu.VMEM((4, SEQ * nq, 128), jnp.float32),
            dma((SLOTS,)), dma((CHUNKS, 2 * NZ)), dma((CHUNKS, NZ)), dma((CHUNKS, NZ)),
            dma((CHUNKS,)), dma((HALVES, 4)), dma((HALVES, 4)),
            dma((2 * NZ,)), dma((2 * NZ,)), dma((4,)), dma((4,)),
        ],
        compiler_params=pltpu.CompilerParams(
            collective_id=0, has_side_effects=True, vmem_limit_bytes=60 << 20),
        cost_estimate=pl.CostEstimate(
            flops=2 * wide * deep * (held + SEQ * nq), bytes_accessed=4 * nq * wide * deep, transcendentals=0),
    )(code, ids, out_factors, in_factors, precond)
    return res[:, :SEQ]


def local_plain(precond, out_factors, in_factors, token_mask, seq_ids, query_ids):
    out_whole = lax.all_gather(out_factors, "col", axis=0, tiled=True)
    in_whole = lax.all_gather(in_factors, "row", axis=0, tiled=True)

    def one_sequence(s):
        weight = ((seq_ids == s) & (token_mask == 1)).astype(jnp.bfloat16)
        outer = lax.dot_general(out_whole, in_whole * weight[:, None], (((0,), (0,)), ((), ())),
                                preferred_element_type=jnp.float32)
        return jnp.sum(precond * outer[None], axis=(1, 2))

    total = lax.map(one_sequence, jnp.arange(SEQ, dtype=jnp.int32))
    raw = lax.psum(total, ("row", "col")).T
    select = (query_ids[:, None] == jnp.arange(raw.shape[0], dtype=jnp.int32)[None, :]).astype(jnp.float32)
    return jnp.dot(select, raw, precision=lax.Precision.HIGHEST) * SCALE


def solution(mesh):
    placed = (P(None, "row", "col"), P("col", "row"), P("row", "col"), P(), P(), P())
    small = mesh.shape["row"] == 4 and mesh.shape["col"] == 2 * NZ
    return jax.shard_map(local_fused if small else local_plain, mesh=mesh, in_specs=placed,
                         out_specs=P(), check_vma=False)
```
